32 devices in a mesh: tp: 8 (over z, x), hb: 4 (over y, core).
Axes of the slice: x: 2, y: 2, z: 4, core: 2. Of those that a mesh axis runs over, the one named last changes fastest.
Arguments:
- normed: bfloat16 [512, 16384], P('hb', 'tp'), may hold values from -6 to 6
- hidden: bfloat16 [512, 26624], P('hb', 'tp'), may hold values from -6 to 6
Outputs:
- h_in: float32 [16384, 16384], P('tp', 'hb')
- h_down: float32 [26624, 3328], P(('tp', 'hb'))
The draws below stay inside these ranges and needn't reach their ends.
All inputs are finite; a program needn't handle non-finite values.
Results may differ from the reference program's by a relative error of at most 0.0003.
Values may be sent and summed in bfloat16 or wider, within the bound.
A program may use at most 192 MiB of HBM per device.

```python
import jax
import jax.numpy as jnp
from jax import lax

D = 16384
FFW = 26624
TOKENS = 512
N_TP = 8


def level_of(stream_key, shape, shards, least, high):
    factor_of = 1.0
    for position, shards_of in shards:
        heights = jax.random.uniform(jax.random.fold_in(jax.random.fold_in(stream_key, 6), position), (shards_of,), jnp.float32, least / len(shards), high / len(shards))
        factor_of = factor_of * jnp.repeat(jnp.exp(heights), shape[position] // shards_of).reshape((-1,) + (1,) * (len(shape) - 1 - position))
    return factor_of


def bell_draw(key, extent, spread, bound, cuts=(), kind=jnp.bfloat16):
    drawn = jax.random.normal(key, extent, jnp.float32) * spread
    if len(cuts) > 0:
        drawn = level_of(key, extent, cuts, -0.22, 0.18) * drawn
    return jnp.clip(drawn, min=-bound, max=bound).astype(kind)


def setup_inputs(seed: int = 0) -> dict:
    streams_of = jax.random.split(jax.random.key(seed), 3)
    normed = bell_draw(streams_of[0], (TOKENS, D), 1.0, 6.0, ((0, 4), (1, 8)))
    hidden = bell_draw(streams_of[1], (TOKENS, FFW), 1.0, 6.0, ((0, 4), (1, 8)))
    return {"normed": normed, "hidden": hidden}


def reference(normed, hidden):
    scale = 2.0 / TOKENS
    rows_in = normed.astype(jnp.float32)
    h_in = jnp.dot(rows_in.T, rows_in, precision=lax.Precision.HIGHEST) * scale
    units = hidden.astype(jnp.float32).reshape(TOKENS, N_TP, FFW // N_TP)
    blocks = jnp.einsum("tbi,tbj->bij", units, units, precision=lax.Precision.HIGHEST)
    h_down = blocks.reshape(FFW, FFW // N_TP) * scale
    return h_in, h_down
```

```python
import functools

import jax
import jax.numpy as jnp
from jax import lax
from jax.experimental import pallas as pl
from jax.experimental.pallas import tpu as pltpu
from jax.sharding import PartitionSpec as P

MESH = pl.DeviceIdType.MESH
PIECES = 4


def gram_product(left, right):
    return lax.dot_general(
        left, right, (((0,), (0,)), ((), ())), preferred_element_type=jnp.float32
    )


def gather_kernel(n_tp, n_hb, normed, hidden, rows, units, cols,
                  local_sem, twin_send, peer_send, pass_send, rows_recv,
                  unit_send, unit_recv, line_send, line_recv, cross_send, cross_recv, own_sem):
    q = n_tp // n_hb
    n_y = n_hb // 2
    t, h = lax.axis_index("tp"), lax.axis_index("hb")
    z, x = t // q, t % q
    y, core = h // 2, h % 2
    twin = y * 2 + 1 - core
    tokens, width = normed.shape
    piece = tokens // PIECES
    n = n_hb * PIECES
    is_source = z == h
    goes_up = jnp.logical_and(z >= h, z < n_hb - 1)
    goes_down = jnp.logical_and(z <= h, z > 0)

    def other_y(d):
        return lax.rem(y + d, n_y) * 2 + core

    def from_y(d):
        return lax.rem(y - d + n_y, n_y) * 2 + core

    def at(group, s):
        return pl.ds(pl.multiple_of(group * tokens + s * piece, piece), piece)

    def block(ref, group):
        return ref.at[pl.ds(pl.multiple_of(group * tokens, tokens), tokens), :]

    def columns(position):
        return pl.ds(pl.multiple_of(position * width, width), width)

    def remote(src, dst, send, recv, where):
        return pltpu.make_async_remote_copy(
            src_ref=src, dst_ref=dst, send_sem=send, recv_sem=recv,
            device_id=where, device_id_type=MESH)

    barrier = pltpu.get_barrier_semaphore()

    def greet(where):
        pl.semaphore_signal(barrier, inc=1, device_id=where, device_id_type=MESH)

    greet({"hb": twin})
    for d in range(1, n_y):
        greet({"hb": other_y(d)})
    for d in range(1, q):
        greet({"tp": z * q + lax.rem(x + d, q)})
    pl.when(z > 0)(lambda: greet({"tp": t - q}))
    pl.when(z < n_hb - 1)(lambda: greet({"tp": t + q}))
    ends = jnp.where(z > 0, 1, 0) + jnp.where(z < n_hb - 1, 1, 0)
    pl.semaphore_wait(barrier, 1 + (n_y - 1) + (q - 1) + ends)

    own_rows = pltpu.make_async_copy(normed, block(rows, h), local_sem.at[0])
    own_units = pltpu.make_async_copy(hidden, block(units, h), local_sem.at[1])

    def own_piece(s):
        return normed.at[pl.ds(pl.multiple_of(s * piece, piece), piece), :]

    def to_twin(s):
        return remote(own_piece(s), rows.at[at(h, s), :], twin_send.at[s],
                      rows_recv.at[h * PIECES + s], {"hb": twin})

    def to_peer(d, s):
        return remote(own_piece(s), rows.at[at(h, s), :], peer_send.at[(d - 1) * PIECES + s],
                      rows_recv.at[h * PIECES + s], {"hb": other_y(d)})

    def pass_on(d, s):
        group = from_y(d)
        return remote(rows.at[at(group, s), :], rows.at[at(group, s), :],
                      pass_send.at[(d - 1) * PIECES + s],
                      rows_recv.at[group * PIECES + s], {"hb": twin})

    def rows_arrival(group, s):
        return remote(own_piece(s), rows.at[at(group, s), :], twin_send.at[s],
                      rows_recv.at[group * PIECES + s], {"hb": twin})

    def units_to(i, where):
        return remote(hidden, block(units, h), unit_send.at[i], unit_recv.at[h], {"hb": where})

    def units_pass(d):
        group = from_y(d)
        return remote(block(units, group), block(units, group), unit_send.at[n_y - 1 + d],
                      unit_recv.at[group], {"hb": twin})

    def units_arrival(group):
        return remote(hidden, block(units, group), unit_send.at[0], unit_recv.at[group],
                      {"hb": twin})

    def place(i):
        k, s = i // PIECES, i % PIECES
        hy, hc = k // 2, k % 2
        group = lax.rem(y + hy, n_y) * 2 + lax.rem(core + hc, 2)
        return group, s

    def line(i, src, step):
        group, s = place(i)
        return remote(src.at[at(group, s), columns(x) if src is cols else slice(None)],
                      cols.at[at(group, s), columns(x)],
                      line_send.at[(0 if step < 0 else n) + i], line_recv.at[i],
                      {"tp": t + step * q})

    def cross(i, src, d):
        group, s = place(i)
        return remote(src.at[at(group, s), columns(x) if src is cols else slice(None)],
                      cols.at[at(group, s), columns(x)],
                      cross_send.at[(d - 1) * n + i], cross_recv.at[(d - 1) * n + i],
                      {"tp": z * q + lax.rem(x + d, q)})

    def cross_arrival(i, d):
        group, s = place(i)
        there = cols.at[at(group, s), columns(lax.rem(x - d + q, q))]
        return remote(there, there, cross_send.at[(d - 1) * n + i],
                      cross_recv.at[(d - 1) * n + i], {"tp": z * q + lax.rem(x + d, q)})

    def own_columns(i):
        group, s = place(i)
        return pltpu.make_async_copy(rows.at[at(group, s), :], cols.at[at(group, s), columns(x)],
                                     own_sem.at[i])

    own_rows.start()
    for d in range(1, n_y):
        for s in range(PIECES):
            to_peer(d, s).start()
    for s in range(PIECES):
        to_twin(s).start()
    own_units.start()
    own_rows.wait()

    def hand_out(i, src):
        pl.when(goes_up)(lambda: line(i, src, 1).start())
        pl.when(goes_down)(lambda: line(i, src, -1).start())
        for d in range(1, q):
            cross(i, src, d).start()

    def step(i):
        group, s = place(i)

        @pl.when(is_source)
        def _():
            awaited = jnp.logical_and(i >= PIECES, (i // PIECES) % 2 == 1)
            pl.when(awaited)(lambda: rows_arrival(group, s).wait_recv())
            hand_out(i, rows)
            own_columns(i).start()

        @pl.when(jnp.logical_not(is_source))
        def _():
            line(i, cols, 1).wait_recv()
            hand_out(i, cols)

    n_first = (n_y - 1) * PIECES

    def first(i, carry):
        step(i)
        d, s = i // PIECES + 1, i % PIECES
        rows_arrival(from_y(d), s).wait_recv()
        pass_on(d, s).start()
        return carry

    def later(i, carry):
        step(i)
        return carry

    lax.fori_loop(0, n_first, first, 0)
    units_to(0, twin).start()
    for d in range(1, n_y):
        units_to(d, other_y(d)).start()
    n_second = max(n_first, n * 3 // 4)
    lax.fori_loop(n_first, n_second, later, 0)
    for d in range(1, n_y):
        units_arrival(from_y(d)).wait_recv()
        units_pass(d).start()
    lax.fori_loop(n_second, n, later, 0)

    def finish_rows(i, carry):
        group, s = place(i)
        pl.when(jnp.logical_and((i // PIECES) % 2 == 1, jnp.logical_not(is_source)))(
            lambda: rows_arrival(group, s).wait_recv())
        return carry

    lax.fori_loop(0, n, finish_rows, 0)
    for k in range(n_y):
        units_arrival(lax.rem(y + k, n_y) * 2 + 1 - core).wait_recv()

    def finish(i, carry):
        for d in range(1, q):
            cross_arrival(i, d).wait_recv()
            cross(i, cols, d).wait_send()
        pl.when(goes_up)(lambda: line(i, cols, 1).wait_send())
        pl.when(goes_down)(lambda: line(i, cols, -1).wait_send())
        pl.when(is_source)(lambda: own_columns(i).wait())
        return carry

    lax.fori_loop(0, n, finish, 0)
    own_units.wait()
    for s in range(PIECES):
        to_twin(s).wait_send()
        for d in range(1, n_y):
            to_peer(d, s).wait_send()
            pass_on(d, s).wait_send()
    units_to(0, twin).wait_send()
    for d in range(1, n_y):
        units_to(d, other_y(d)).wait_send()
        units_pass(d).wait_send()


def gather(normed, hidden):
    n_tp, n_hb = lax.axis_size("tp"), lax.axis_size("hb")
    q, n_y = n_tp // n_hb, n_hb // 2
    tokens, width = normed.shape
    n = n_hb * PIECES
    dma = pltpu.SemaphoreType.DMA
    anywhere = pl.BlockSpec(memory_space=pl.ANY)
    far = max(1, (n_y - 1) * PIECES)
    return pl.pallas_call(
        functools.partial(gather_kernel, n_tp, n_hb),
        out_shape=(
            jax.ShapeDtypeStruct((n_hb * tokens, width), normed.dtype),
            jax.ShapeDtypeStruct((n_hb * tokens, hidden.shape[1]), hidden.dtype),
            jax.ShapeDtypeStruct((n_hb * tokens, q * width), normed.dtype),
        ),
        in_specs=[anywhere] * 2,
        out_specs=(anywhere,) * 3,
        scratch_shapes=[
            dma((2,)), dma((PIECES,)), dma((far,)), dma((far,)), dma((n,)),
            dma((2 * n_y,)), dma((n_hb,)), dma((2 * n,)), dma((n,)),
            dma((max(1, q - 1) * n,)), dma((max(1, q - 1) * n,)), dma((n,)),
        ],
        compiler_params=pltpu.CompilerParams(collective_id=0, has_side_effects=True),
    )(normed, hidden)


def per_device(normed, hidden):
    groups = lax.axis_size("hb")
    scale = 2.0 / (normed.shape[0] * groups)
    rows, units, cols = gather(normed, hidden)
    h_in = gram_product(rows, cols) * scale
    own = hidden.shape[1] // groups
    mine = lax.dynamic_slice_in_dim(units, lax.axis_index("hb") * own, own, axis=1)
    h_down = gram_product(mine, units) * scale
    return (h_in, h_down)


def solution(mesh):
    return jax.shard_map(
        per_device,
        mesh=mesh,
        in_specs=(P("hb", "tp"), P("hb", "tp")),
        out_specs=(P("tp", "hb"), P(("tp", "hb"), None)),
        check_vma=False,
    )
```

```python
import functools

import jax
import jax.numpy as jnp
from jax import lax
from jax.experimental import pallas as pl
from jax.experimental.pallas import tpu as pltpu
from jax.sharding import PartitionSpec as P

MESH = pl.DeviceIdType.MESH
PIECES = 4


def gather_kernel(n_tp, n_hb, normed, hidden, rows, units, cols,
                  local_sem, twin_send, peer_send, pass_send, rows_recv,
                  unit_send, unit_recv, line_send, line_recv, cross_send, cross_recv, own_sem):
    q = n_tp // n_hb
    n_y = n_hb // 2
    t, h = lax.axis_index("tp"), lax.axis_index("hb")
    z, x = t // q, t % q
    y, core = h // 2, h % 2
    twin = y * 2 + 1 - core
    tokens, width = normed.shape
    piece = tokens // PIECES
    n = n_hb * PIECES
    is_source = z == h
    goes_up = jnp.logical_and(z >= h, z < n_hb - 1)
    goes_down = jnp.logical_and(z <= h, z > 0)

    def other_y(d):
        return lax.rem(y + d, n_y) * 2 + core

    def from_y(d):
        return lax.rem(y - d + n_y, n_y) * 2 + core

    def at(group, s):
        return pl.ds(pl.multiple_of(group * tokens + s * piece, piece), piece)

    def block(ref, group):
        return ref.at[pl.ds(pl.multiple_of(group * tokens, tokens), tokens), :]

    def columns(position):
        return pl.ds(pl.multiple_of(position * width, width), width)

    def remote(src, dst, send, recv, where):
        return pltpu.make_async_remote_copy(
            src_ref=src, dst_ref=dst, send_sem=send, recv_sem=recv,
            device_id=where, device_id_type=MESH)

    barrier = pltpu.get_barrier_semaphore()

    def greet(where):
        pl.semaphore_signal(barrier, inc=1, device_id=where, device_id_type=MESH)

    greet({"hb": twin})
    for d in range(1, n_y):
        greet({"hb": other_y(d)})
    for d in range(1, q):
        greet({"tp": z * q + lax.rem(x + d, q)})
    pl.when(z > 0)(lambda: greet({"tp": t - q}))
    pl.when(z < n_hb - 1)(lambda: greet({"tp": t + q}))
    ends = jnp.where(z > 0, 1, 0) + jnp.where(z < n_hb - 1, 1, 0)
    pl.semaphore_wait(barrier, 1 + (n_y - 1) + (q - 1) + ends)

    own_rows = pltpu.make_async_copy(normed, block(rows, h), local_sem.at[0])
    own_units = pltpu.make_async_copy(hidden, block(units, h), local_sem.at[1])

    def own_piece(s):
        return normed.at[pl.ds(pl.multiple_of(s * piece, piece), piece), :]

    def to_twin(s):
        return remote(own_piece(s), rows.at[at(h, s), :], twin_send.at[s],
                      rows_recv.at[h * PIECES + s], {"hb": twin})

    def to_peer(d, s):
        return remote(own_piece(s), rows.at[at(h, s), :], peer_send.at[(d - 1) * PIECES + s],
                      rows_recv.at[h * PIECES + s], {"hb": other_y(d)})

    def pass_on(d, s):
        group = from_y(d)
        return remote(rows.at[at(group, s), :], rows.at[at(group, s), :],
                      pass_send.at[(d - 1) * PIECES + s],
                      rows_recv.at[group * PIECES + s], {"hb": twin})

    def rows_arrival(group, s):
        return remote(own_piece(s), rows.at[at(group, s), :], twin_send.at[s],
                      rows_recv.at[group * PIECES + s], {"hb": twin})

    def units_to(i, where):
        return remote(hidden, block(units, h), unit_send.at[i], unit_recv.at[h], {"hb": where})

    def units_pass(d):
        group = from_y(d)
        return remote(block(units, group), block(units, group), unit_send.at[n_y - 1 + d],
                      unit_recv.at[group], {"hb": twin})

    def units_arrival(group):
        return remote(hidden, block(units, group), unit_send.at[0], unit_recv.at[group],
                      {"hb": twin})

    def place(i):
        k, s = i // PIECES, i % PIECES
        hy, hc = k // 2, k % 2
        group = lax.rem(y + hy, n_y) * 2 + lax.rem(core + hc, 2)
        return group, s

    def line(i, src, step):
        group, s = place(i)
        return remote(src.at[at(group, s), columns(x) if src is cols else slice(None)],
                      cols.at[at(group, s), columns(x)],
                      line_send.at[(0 if step < 0 else n) + i], line_recv.at[i],
                      {"tp": t + step * q})

    def cross(i, src, d):
        group, s = place(i)
        return remote(src.at[at(group, s), columns(x) if src is cols else slice(None)],
                      cols.at[at(group, s), columns(x)],
                      cross_send.at[(d - 1) * n + i], cross_recv.at[(d - 1) * n + i],
                      {"tp": z * q + lax.rem(x + d, q)})

    def cross_arrival(i, d):
        group, s = place(i)
        there = cols.at[at(group, s), columns(lax.rem(x - d + q, q))]
        return remote(there, there, cross_send.at[(d - 1) * n + i],
                      cross_recv.at[(d - 1) * n + i], {"tp": z * q + lax.rem(x + d, q)})

    def own_columns(i):
        group, s = place(i)
        return pltpu.make_async_copy(rows.at[at(group, s), :], cols.at[at(group, s), columns(x)],
                                     own_sem.at[i])

    own_rows.start()
    for d in range(1, n_y):
        for s in range(PIECES):
            to_peer(d, s).start()
    for s in range(PIECES):
        to_twin(s).start()
    own_units.start()
    own_rows.wait()

    def hand_out(i, src):
        pl.when(goes_up)(lambda: line(i, src, 1).start())
        pl.when(goes_down)(lambda: line(i, src, -1).start())
        for d in range(1, q):
            cross(i, src, d).start()

    def step(i):
        group, s = place(i)

        @pl.when(is_source)
        def _():
            awaited = jnp.logical_and(i >= PIECES, (i // PIECES) % 2 == 1)
            pl.when(awaited)(lambda: rows_arrival(group, s).wait_recv())
            hand_out(i, rows)
            own_columns(i).start()

        @pl.when(jnp.logical_not(is_source))
        def _():
            line(i, cols, 1).wait_recv()
            hand_out(i, cols)

    n_first = (n_y - 1) * PIECES

    def first(i, carry):
        step(i)
        d, s = i // PIECES + 1, i % PIECES
        rows_arrival(from_y(d), s).wait_recv()
        pass_on(d, s).start()
        return carry

    def later(i, carry):
        step(i)
        return carry

    lax.fori_loop(0, n_first, first, 0)
    units_to(0, twin).start()
    for d in range(1, n_y):
        units_to(d, other_y(d)).start()
    n_second = max(n_first, n * 3 // 4)
    lax.fori_loop(n_first, n_second, later, 0)
    for d in range(1, n_y):
        units_arrival(from_y(d)).wait_recv()
        units_pass(d).start()
    lax.fori_loop(n_second, n, later, 0)

    def finish_rows(i, carry):
        group, s = place(i)
        pl.when(jnp.logical_and((i // PIECES) % 2 == 1, jnp.logical_not(is_source)))(
            lambda: rows_arrival(group, s).wait_recv())
        return carry

    lax.fori_loop(0, n, finish_rows, 0)
    for k in range(n_y):
        units_arrival(lax.rem(y + k, n_y) * 2 + 1 - core).wait_recv()

    def finish(i, carry):
        for d in range(1, q):
            cross_arrival(i, d).wait_recv()
            cross(i, cols, d).wait_send()
        pl.when(goes_up)(lambda: line(i, cols, 1).wait_send())
        pl.when(goes_down)(lambda: line(i, cols, -1).wait_send())
        pl.when(is_source)(lambda: own_columns(i).wait())
        return carry

    lax.fori_loop(0, n, finish, 0)
    own_units.wait()
    for s in range(PIECES):
        to_twin(s).wait_send()
        for d in range(1, n_y):
            to_peer(d, s).wait_send()
            pass_on(d, s).wait_send()
    units_to(0, twin).wait_send()
    for d in range(1, n_y):
        units_to(d, other_y(d)).wait_send()
        units_pass(d).wait_send()


def gather(normed, hidden):
    n_tp, n_hb = lax.axis_size("tp"), lax.axis_size("hb")
    q, n_y = n_tp // n_hb, n_hb // 2
    tokens, width = normed.shape
    n = n_hb * PIECES
    dma = pltpu.SemaphoreType.DMA
    anywhere = pl.BlockSpec(memory_space=pl.ANY)
    far = max(1, (n_y - 1) * PIECES)
    return pl.pallas_call(
        functools.partial(gather_kernel, n_tp, n_hb),
        out_shape=(
            jax.ShapeDtypeStruct((n_hb * tokens, width), normed.dtype),
            jax.ShapeDtypeStruct((n_hb * tokens, hidden.shape[1]), hidden.dtype),
            jax.ShapeDtypeStruct((n_hb * tokens, q * width), normed.dtype),
        ),
        in_specs=[anywhere] * 2,
        out_specs=(anywhere,) * 3,
        scratch_shapes=[
            dma((2,)), dma((PIECES,)), dma((far,)), dma((far,)), dma((n,)),
            dma((2 * n_y,)), dma((n_hb,)), dma((2 * n,)), dma((n,)),
            dma((max(1, q - 1) * n,)), dma((max(1, q - 1) * n,)), dma((n,)),
        ],
        compiler_params=pltpu.CompilerParams(collective_id=0, has_side_effects=True),
    )(normed, hidden)


def tile_of(width):
    return 256 if width % 256 == 0 else 128


def window_of(own, width):
    return min(width, -(-(own + 120) // 128) * 128)


def product_kernel(n_down, scale, rows, units_tile, units, cols_tile, down, h_in,
                   rows_in, rows_t, window, window_t, mine_t, sem):
    i = pl.program_id(0)
    width = units.shape[1]
    own, span = mine_t.shape[0], window.shape[1]
    first = lax.axis_index("hb") * own
    start = jnp.minimum(first // 128 * 128, width - span)
    get_window = pltpu.make_async_copy(
        units.at[:, pl.ds(pl.multiple_of(start, 128), span)], window, sem.at[0])
    get_rows = pltpu.make_async_copy(rows, rows_in, sem.at[1])

    @pl.when(i == 0)
    def _():
        get_window.start()
        get_rows.start()
        get_window.wait()
        window_t[...] = window[...].T.astype(jnp.float32)
        mine_t[...] = window_t[pl.ds(pl.multiple_of(first - start, 8), own), :].astype(mine_t.dtype)

    @pl.when(i < n_down)
    def _():
        down[...] = scale * jnp.dot(
            mine_t[...], units_tile[...], preferred_element_type=jnp.float32)

    @pl.when(i == n_down)
    def _():
        get_rows.wait()
        rows_t[...] = rows_in[...].T

    @pl.when(i >= n_down)
    def _():
        h_in[...] = scale * jnp.dot(
            rows_t[...], cols_tile[...], preferred_element_type=jnp.float32)


def products(rows, units, cols, scale):
    n_hb = lax.axis_size("hb")
    tokens, high = rows.shape
    own = units.shape[1] // n_hb
    down_tile, in_tile = tile_of(units.shape[1]), tile_of(cols.shape[1])
    n_down, n_in = units.shape[1] // down_tile, cols.shape[1] // in_tile
    span = window_of(own, units.shape[1])
    anywhere = pl.BlockSpec(memory_space=pl.ANY)
    early = lambda i: (0, jnp.minimum(i, n_down - 1))
    late = lambda i: (0, jnp.maximum(i - n_down, 0))
    return pl.pallas_call(
        functools.partial(product_kernel, n_down, scale),
        grid=(n_down + n_in,),
        out_shape=(
            jax.ShapeDtypeStruct((own, units.shape[1]), jnp.float32),
            jax.ShapeDtypeStruct((high, cols.shape[1]), jnp.float32),
        ),
        in_specs=[
            anywhere,
            pl.BlockSpec((tokens, down_tile), early),
            anywhere,
            pl.BlockSpec((tokens, in_tile), late),
        ],
        out_specs=(
            pl.BlockSpec((own, down_tile), early),
            pl.BlockSpec((high, in_tile), late),
        ),
        scratch_shapes=[
            pltpu.VMEM((tokens, high), rows.dtype),
            pltpu.VMEM((high, tokens), rows.dtype),
            pltpu.VMEM((tokens, span), units.dtype),
            pltpu.VMEM((span, tokens), jnp.float32),
            pltpu.VMEM((own, tokens), units.dtype),
            pltpu.SemaphoreType.DMA((2,)),
        ],
        compiler_params=pltpu.CompilerParams(vmem_limit_bytes=40 * 2**20),
    )(rows, units, units, cols)


def per_device(normed, hidden):
    scale = 2.0 / (normed.shape[0] * lax.axis_size("hb"))
    rows, units, cols = gather(normed, hidden)
    h_down, h_in = products(rows, units, cols, scale)
    return (h_in, h_down)


def solution(mesh):
    return jax.shard_map(
        per_device,
        mesh=mesh,
        in_specs=(P("hb", "tp"), P("hb", "tp")),
        out_specs=(P("tp", "hb"), P(("tp", "hb"), None)),
        check_vma=False,
    )
```

```python
import functools

import jax
import jax.numpy as jnp
from jax import lax
from jax.experimental import pallas as pl
from jax.experimental.pallas import tpu as pltpu
from jax.sharding import PartitionSpec as P

MESH = pl.DeviceIdType.MESH
PIECES = 4


def tile_of(width):
    return 256 if width % 256 == 0 else 128


def window_of(own, width):
    return min(width, -(-(own + 120) // 128) * 128)


def gather_kernel(n_tp, n_hb, scale, normed, hidden, rows_out, mine_out, units_out, cols_out,
                  rows, units, cols, rows_t, window_t, mine_t,
                  local_sem, twin_send, peer_send, pass_send, rows_recv,
                  unit_send, unit_recv, line_send, line_recv, cross_send, cross_recv,
                  out_sem, cross_out_sem):
    q = n_tp // n_hb
    n_y = n_hb // 2
    t, h = lax.axis_index("tp"), lax.axis_index("hb")
    z, x = t // q, t % q
    y, core = h // 2, h % 2
    twin = y * 2 + 1 - core
    tokens, width = normed.shape
    piece = tokens // PIECES
    n = n_hb * PIECES
    is_source = z == h
    goes_up = jnp.logical_and(z >= h, z < n_hb - 1)
    goes_down = jnp.logical_and(z <= h, z > 0)

    def other_y(d):
        return lax.rem(y + d, n_y) * 2 + core

    def from_y(d):
        return lax.rem(y - d + n_y, n_y) * 2 + core

    def at(group, s):
        return pl.ds(pl.multiple_of(group * tokens + s * piece, piece), piece)

    def block(ref, group):
        return ref.at[pl.ds(pl.multiple_of(group * tokens, tokens), tokens), :]

    def columns(position):
        return pl.ds(pl.multiple_of(position * width, width), width)

    def remote(src, dst, send, recv, where):
        return pltpu.make_async_remote_copy(
            src_ref=src, dst_ref=dst, send_sem=send, recv_sem=recv,
            device_id=where, device_id_type=MESH)

    barrier = pltpu.get_barrier_semaphore()

    def greet(where):
        pl.semaphore_signal(barrier, inc=1, device_id=where, device_id_type=MESH)

    greet({"hb": twin})
    for d in range(1, n_y):
        greet({"hb": other_y(d)})
    for d in range(1, q):
        greet({"tp": z * q + lax.rem(x + d, q)})
    pl.when(z > 0)(lambda: greet({"tp": t - q}))
    pl.when(z < n_hb - 1)(lambda: greet({"tp": t + q}))
    ends = jnp.where(z > 0, 1, 0) + jnp.where(z < n_hb - 1, 1, 0)
    pl.semaphore_wait(barrier, 1 + (n_y - 1) + (q - 1) + ends)

    own_rows = pltpu.make_async_copy(normed, block(rows, h), local_sem.at[0])
    own_units = pltpu.make_async_copy(hidden, block(units, h), local_sem.at[1])

    def own_piece(s):
        return normed.at[pl.ds(pl.multiple_of(s * piece, piece), piece), :]

    def to_twin(s):
        return remote(own_piece(s), rows.at[at(h, s), :], twin_send.at[s],
                      rows_recv.at[h * PIECES + s], {"hb": twin})

    def to_peer(d, s):
        return remote(own_piece(s), rows.at[at(h, s), :], peer_send.at[(d - 1) * PIECES + s],
                      rows_recv.at[h * PIECES + s], {"hb": other_y(d)})

    def pass_on(d, s):
        group = from_y(d)
        return remote(rows.at[at(group, s), :], rows.at[at(group, s), :],
                      pass_send.at[(d - 1) * PIECES + s],
                      rows_recv.at[group * PIECES + s], {"hb": twin})

    def rows_arrival(group, s):
        return remote(own_piece(s), rows.at[at(group, s), :], twin_send.at[s],
                      rows_recv.at[group * PIECES + s], {"hb": twin})

    def units_to(i, where):
        return remote(hidden, block(units, h), unit_send.at[i], unit_recv.at[h], {"hb": where})

    def units_pass(d):
        group = from_y(d)
        return remote(block(units, group), block(units, group), unit_send.at[n_y - 1 + d],
                      unit_recv.at[group], {"hb": twin})

    def units_arrival(group):
        return remote(hidden, block(units, group), unit_send.at[0], unit_recv.at[group],
                      {"hb": twin})

    def place(i):
        k, s = i // PIECES, i % PIECES
        hy, hc = k // 2, k % 2
        group = lax.rem(y + hy, n_y) * 2 + lax.rem(core + hc, 2)
        return group, s

    def line(i, src, step):
        group, s = place(i)
        return remote(src.at[at(group, s), columns(x) if src is cols else slice(None)],
                      cols.at[at(group, s), columns(x)],
                      line_send.at[(0 if step < 0 else n) + i], line_recv.at[i],
                      {"tp": t + step * q})

    def cross(i, src, d):
        group, s = place(i)
        return remote(src.at[at(group, s), columns(x) if src is cols else slice(None)],
                      cols.at[at(group, s), columns(x)],
                      cross_send.at[(d - 1) * n + i], cross_recv.at[(d - 1) * n + i],
                      {"tp": z * q + lax.rem(x + d, q)})

    def cross_arrival(i, d):
        group, s = place(i)
        there = cols.at[at(group, s), columns(lax.rem(x - d + q, q))]
        return remote(there, there, cross_send.at[(d - 1) * n + i],
                      cross_recv.at[(d - 1) * n + i], {"tp": z * q + lax.rem(x + d, q)})

    def columns_out(i):
        group, s = place(i)
        there = at(group, s), columns(x)
        return pltpu.make_async_copy(cols.at[there], cols_out.at[there], out_sem.at[i])

    def own_columns_out(i):
        group, s = place(i)
        return pltpu.make_async_copy(rows.at[at(group, s), :],
                                     cols_out.at[at(group, s), columns(x)], out_sem.at[i])

    def cross_out(i, d):
        group, s = place(i)
        there = at(group, s), columns(lax.rem(x - d + q, q))
        return pltpu.make_async_copy(cols.at[there], cols_out.at[there],
                                     cross_out_sem.at[(d - 1) * n + i])

    rows_done = pltpu.make_async_copy(rows_t, rows_out, local_sem.at[2])
    mine_done = pltpu.make_async_copy(mine_t, mine_out, local_sem.at[3])
    units_done = pltpu.make_async_copy(units, units_out, local_sem.at[4])

    own_rows.start()
    for d in range(1, n_y):
        for s in range(PIECES):
            to_peer(d, s).start()
    for s in range(PIECES):
        to_twin(s).start()
    own_units.start()
    own_rows.wait()

    tile = tile_of(width)
    n_turns = width // tile
    factor = jnp.asarray(scale, rows_t.dtype)

    def hand_out(i, src):
        pl.when(goes_up)(lambda: line(i, src, 1).start())
        pl.when(goes_down)(lambda: line(i, src, -1).start())
        for d in range(1, q):
            cross(i, src, d).start()

    def step(i):
        group, s = place(i)

        @pl.when(is_source)
        def _():
            awaited = jnp.logical_and(i < n - n_turns, (i // PIECES) % 2 == 1)
            pl.when(awaited)(lambda: rows_arrival(group, s).wait_recv())
            hand_out(i, rows)
            own_columns_out(i).start()

        @pl.when(jnp.logical_not(is_source))
        def _():
            line(i, cols, 1).wait_recv()
            hand_out(i, cols)
            columns_out(i).start()

    n_first = (n_y - 1) * PIECES

    def first(i, carry):
        step(i)
        d, s = i // PIECES + 1, i % PIECES
        rows_arrival(from_y(d), s).wait_recv()
        pass_on(d, s).start()
        return carry

    def later(i, carry):
        step(i)
        return carry

    lax.fori_loop(0, n_first, first, 0)
    units_to(0, twin).start()
    for d in range(1, n_y):
        units_to(d, other_y(d)).start()

    def finish_rows(i, carry):
        group, s = place(i)
        pl.when(jnp.logical_and((i // PIECES) % 2 == 1,
                                jnp.logical_or(jnp.logical_not(is_source), i >= n - n_turns)))(
            lambda: rows_arrival(group, s).wait_recv())
        return carry

    def turn(b):
        part = pl.ds(pl.multiple_of(b * tile, tile), tile)
        rows_t[part, :] = (rows[:, part].T * factor).astype(rows_t.dtype)

    def last(i, carry):
        step(i)
        turn(i - (n - n_turns))
        return carry

    lax.fori_loop(n_first, n - n_turns, later, 0)
    lax.fori_loop(0, n, finish_rows, 0)
    middle = n - max(1, n_turns // 2)
    lax.fori_loop(n - n_turns, middle, last, 0)
    for d in range(1, n_y):
        units_arrival(from_y(d)).wait_recv()
        units_pass(d).start()
    lax.fori_loop(middle, n, last, 0)
    rows_done.start()

    for k in range(n_y):
        units_arrival(lax.rem(y + k, n_y) * 2 + 1 - core).wait_recv()
    own_units.wait()
    units_done.start()
    own, span = mine_t.shape[0], window_t.shape[0]
    first_column = h * own
    start = jnp.minimum(first_column // 128 * 128, units.shape[1] - span)

    def turn_units(b, carry):
        there = pl.ds(pl.multiple_of(start + b * 128, 128), 128)
        window_t[pl.ds(pl.multiple_of(b * 128, 128), 128), :] = (
            units[:, there].T.astype(jnp.float32) * scale)
        return carry

    lax.fori_loop(0, span // 128, turn_units, 0)
    mine_t[...] = window_t[pl.ds(pl.multiple_of(first_column - start, 8), own), :].astype(
        mine_t.dtype)
    mine_done.start()

    def finish(i, carry):
        for d in range(1, q):
            cross_arrival(i, d).wait_recv()
            cross_out(i, d).start()
        return carry

    def finish_sends(i, carry):
        for d in range(1, q):
            cross(i, cols, d).wait_send()
            cross_out(i, d).wait()
        pl.when(goes_up)(lambda: line(i, cols, 1).wait_send())
        pl.when(goes_down)(lambda: line(i, cols, -1).wait_send())
        columns_out(i).wait()
        return carry

    lax.fori_loop(0, n, finish, 0)
    lax.fori_loop(0, n, finish_sends, 0)
    rows_done.wait()
    mine_done.wait()
    units_done.wait()
    for s in range(PIECES):
        to_twin(s).wait_send()
        for d in range(1, n_y):
            to_peer(d, s).wait_send()
            pass_on(d, s).wait_send()
    units_to(0, twin).wait_send()
    for d in range(1, n_y):
        units_to(d, other_y(d)).wait_send()
        units_pass(d).wait_send()


def gather(normed, hidden, scale):
    n_tp, n_hb = lax.axis_size("tp"), lax.axis_size("hb")
    q, n_y = n_tp // n_hb, n_hb // 2
    tokens, width = normed.shape
    units = hidden.shape[1]
    own = units // n_hb
    total = n_hb * tokens
    n = n_hb * PIECES
    dma = pltpu.SemaphoreType.DMA
    anywhere = pl.BlockSpec(memory_space=pltpu.HBM)
    far = max(1, (n_y - 1) * PIECES)
    crossings = max(1, q - 1) * n
    kind = normed.dtype
    return pl.pallas_call(
        functools.partial(gather_kernel, n_tp, n_hb, scale),
        out_shape=(
            jax.ShapeDtypeStruct((width, total), kind),
            jax.ShapeDtypeStruct((own, total), kind),
            jax.ShapeDtypeStruct((total, units), kind),
            jax.ShapeDtypeStruct((total, q * width), kind),
        ),
        in_specs=[anywhere] * 2,
        out_specs=(anywhere,) * 4,
        scratch_shapes=[
            pltpu.VMEM((total, width), kind),
            pltpu.VMEM((total, units), kind),
            pltpu.VMEM((total, q * width), kind),
            pltpu.VMEM((width, total), kind),
            pltpu.VMEM((window_of(own, units), total), jnp.float32),
            pltpu.VMEM((own, total), kind),
            dma((5,)), dma((PIECES,)), dma((far,)), dma((far,)), dma((n,)),
            dma((2 * n_y,)), dma((n_hb,)), dma((2 * n,)), dma((n,)),
            dma((crossings,)), dma((crossings,)), dma((n,)), dma((crossings,)),
        ],
        compiler_params=pltpu.CompilerParams(
            collective_id=0, has_side_effects=True, vmem_limit_bytes=60 * 2**20),
    )(normed, hidden)


def product_kernel(n_down, mine_t, units_tile, rows_t, cols_tile, down, h_in, rows_in, sem):
    i = pl.program_id(0)
    get_rows = pltpu.make_async_copy(rows_t, rows_in, sem)
    pl.when(i == 0)(get_rows.start)

    @pl.when(i < n_down)
    def _():
        down[...] = jnp.dot(mine_t[...], units_tile[...], preferred_element_type=jnp.float32)

    pl.when(i == n_down)(get_rows.wait)

    @pl.when(i >= n_down)
    def _():
        h_in[...] = jnp.dot(rows_in[...], cols_tile[...], preferred_element_type=jnp.float32)


def products(rows_t, mine_t, units, cols):
    own, tokens = mine_t.shape
    high = rows_t.shape[0]
    down_tile, in_tile = tile_of(units.shape[1]), tile_of(cols.shape[1])
    n_down, n_in = units.shape[1] // down_tile, cols.shape[1] // in_tile
    early = lambda i: (0, jnp.minimum(i, n_down - 1))
    late = lambda i: (0, jnp.maximum(i - n_down, 0))
    return pl.pallas_call(
        functools.partial(product_kernel, n_down),
        grid=(n_down + n_in,),
        out_shape=(
            jax.ShapeDtypeStruct((own, units.shape[1]), jnp.float32),
            jax.ShapeDtypeStruct((high, cols.shape[1]), jnp.float32),
        ),
        in_specs=[
            pl.BlockSpec((own, tokens), lambda i: (0, 0)),
            pl.BlockSpec((tokens, down_tile), early),
            pl.BlockSpec(memory_space=pltpu.HBM),
            pl.BlockSpec((tokens, in_tile), late),
        ],
        out_specs=(
            pl.BlockSpec((own, down_tile), early),
            pl.BlockSpec((high, in_tile), late),
        ),
        scratch_shapes=[pltpu.VMEM((high, tokens), rows_t.dtype), pltpu.SemaphoreType.DMA],
        compiler_params=pltpu.CompilerParams(vmem_limit_bytes=60 * 2**20),
    )(mine_t, units, rows_t, cols)


def per_device(normed, hidden):
    total = normed.shape[0] * lax.axis_size("hb")
    assert total & (total - 1) == 0
    rows_t, mine_t, units, cols = gather(normed, hidden, 2.0 / total)
    h_down, h_in = products(rows_t, mine_t, units, cols)
    return (h_in, h_down)


def solution(mesh):
    return jax.shard_map(
        per_device,
        mesh=mesh,
        in_specs=(P("hb", "tp"), P("hb", "tp")),
        out_specs=(P("tp", "hb"), P(("tp", "hb"), None)),
        check_vma=False,
    )
```

```python
import functools

import jax
import jax.numpy as jnp
from jax import lax
from jax.experimental import pallas as pl
from jax.experimental.pallas import tpu as pltpu
from jax.sharding import PartitionSpec as P

MESH = pl.DeviceIdType.MESH
PIECES = 4


def tile_of(width):
    return 256 if width % 256 == 0 else 128


def window_of(own, width):
    return min(width, -(-(own + 120) // 128) * 128)


def gather_kernel(n_tp, n_hb, scale, normed, hidden, rows_out, mine_out, units_out, cols_out,
                  rows, units, cols, rows_t, window_t, mine_t,
                  local_sem, twin_send, peer_send, pass_send, rows_recv,
                  unit_send, unit_recv, line_send, line_recv, cross_send, cross_recv,
                  out_sem, cross_out_sem):
    q = n_tp // n_hb
    n_y = n_hb // 2
    t, h = lax.axis_index("tp"), lax.axis_index("hb")
    z, x = t // q, t % q
    y, core = h // 2, h % 2
    twin = y * 2 + 1 - core
    tokens, width = normed.shape
    piece = tokens // PIECES
    n = n_hb * PIECES
    is_source = z == h
    goes_up = jnp.logical_and(z >= h, z < n_hb - 1)
    goes_down = jnp.logical_and(z <= h, z > 0)

    def other_y(d):
        return lax.rem(y + d, n_y) * 2 + core

    def from_y(d):
        return lax.rem(y - d + n_y, n_y) * 2 + core

    def at(group, s):
        return pl.ds(pl.multiple_of(group * tokens + s * piece, piece), piece)

    def block(ref, group):
        return ref.at[pl.ds(pl.multiple_of(group * tokens, tokens), tokens), :]

    def columns(position):
        return pl.ds(pl.multiple_of(position * width, width), width)

    def remote(src, dst, send, recv, where):
        return pltpu.make_async_remote_copy(
            src_ref=src, dst_ref=dst, send_sem=send, recv_sem=recv,
            device_id=where, device_id_type=MESH)

    barrier = pltpu.get_barrier_semaphore()

    def greet(where):
        pl.semaphore_signal(barrier, inc=1, device_id=where, device_id_type=MESH)

    greet({"hb": twin})
    for d in range(1, n_y):
        greet({"hb": other_y(d)})
    for d in range(1, q):
        greet({"tp": z * q + lax.rem(x + d, q)})
    pl.when(z > 0)(lambda: greet({"tp": t - q}))
    pl.when(z < n_hb - 1)(lambda: greet({"tp": t + q}))
    ends = jnp.where(z > 0, 1, 0) + jnp.where(z < n_hb - 1, 1, 0)
    pl.semaphore_wait(barrier, 1 + (n_y - 1) + (q - 1) + ends)

    own_rows = pltpu.make_async_copy(normed, block(rows, h), local_sem.at[0])
    own_units = pltpu.make_async_copy(hidden, block(units, h), local_sem.at[1])

    def own_piece(s):
        return normed.at[pl.ds(pl.multiple_of(s * piece, piece), piece), :]

    def to_twin(s):
        return remote(own_piece(s), rows.at[at(h, s), :], twin_send.at[s],
                      rows_recv.at[h * PIECES + s], {"hb": twin})

    def to_peer(d, s):
        return remote(own_piece(s), rows.at[at(h, s), :], peer_send.at[(d - 1) * PIECES + s],
                      rows_recv.at[h * PIECES + s], {"hb": other_y(d)})

    def pass_on(d, s):
        group = from_y(d)
        return remote(rows.at[at(group, s), :], rows.at[at(group, s), :],
                      pass_send.at[(d - 1) * PIECES + s],
                      rows_recv.at[group * PIECES + s], {"hb": twin})

    def rows_arrival(group, s):
        return remote(own_piece(s), rows.at[at(group, s), :], twin_send.at[s],
                      rows_recv.at[group * PIECES + s], {"hb": twin})

    def units_to(i, where):
        return remote(hidden, block(units, h), unit_send.at[i], unit_recv.at[h], {"hb": where})

    def units_pass(d):
        group = from_y(d)
        return remote(block(units, group), block(units, group), unit_send.at[n_y - 1 + d],
                      unit_recv.at[group], {"hb": twin})

    def units_arrival(group):
        return remote(hidden, block(units, group), unit_send.at[0], unit_recv.at[group],
                      {"hb": twin})

    def place(i):
        k, s = i // PIECES, i % PIECES
        hy, hc = k // 2, k % 2
        group = lax.rem(y + hy, n_y) * 2 + lax.rem(core + hc, 2)
        return group, s

    def line(i, src, step):
        group, s = place(i)
        return remote(src.at[at(group, s), columns(x) if src is cols else slice(None)],
                      cols.at[at(group, s), columns(x)],
                      line_send.at[(0 if step < 0 else n) + i], line_recv.at[i],
                      {"tp": t + step * q})

    def cross(i, src, d):
        group, s = place(i)
        return remote(src.at[at(group, s), columns(x) if src is cols else slice(None)],
                      cols.at[at(group, s), columns(x)],
                      cross_send.at[(d - 1) * n + i], cross_recv.at[(d - 1) * n + i],
                      {"tp": z * q + lax.rem(x + d, q)})

    def cross_arrival(i, d):
        group, s = place(i)
        there = cols.at[at(group, s), columns(lax.rem(x - d + q, q))]
        return remote(there, there, cross_send.at[(d - 1) * n + i],
                      cross_recv.at[(d - 1) * n + i], {"tp": z * q + lax.rem(x + d, q)})

    def columns_out(i):
        group, s = place(i)
        there = at(group, s), columns(x)
        return pltpu.make_async_copy(cols.at[there], cols_out.at[there], out_sem.at[i])

    def own_columns_out(i):
        group, s = place(i)
        return pltpu.make_async_copy(rows.at[at(group, s), :],
                                     cols_out.at[at(group, s), columns(x)], out_sem.at[i])

    def cross_out(i, d):
        group, s = place(i)
        there = at(group, s), columns(lax.rem(x - d + q, q))
        return pltpu.make_async_copy(cols.at[there], cols_out.at[there],
                                     cross_out_sem.at[(d - 1) * n + i])

    rows_done = pltpu.make_async_copy(rows_t, rows_out, local_sem.at[2])
    mine_done = pltpu.make_async_copy(mine_t, mine_out, local_sem.at[3])
    units_done = pltpu.make_async_copy(units, units_out, local_sem.at[4])

    own_rows.start()
    for d in range(1, n_y):
        for s in range(PIECES):
            to_peer(d, s).start()
    for s in range(PIECES):
        to_twin(s).start()
    own_units.start()
    own_rows.wait()

    tile = tile_of(width)
    n_turns = width // tile
    factor = jnp.asarray(scale, rows_t.dtype)

    def hand_out(i, src):
        pl.when(goes_up)(lambda: line(i, src, 1).start())
        pl.when(goes_down)(lambda: line(i, src, -1).start())
        for d in range(1, q):
            cross(i, src, d).start()

    def step(i):
        group, s = place(i)

        @pl.when(is_source)
        def _():
            awaited = jnp.logical_and(i < n - n_turns, (i // PIECES) % 2 == 1)
            pl.when(awaited)(lambda: rows_arrival(group, s).wait_recv())
            hand_out(i, rows)
            own_columns_out(i).start()

        @pl.when(jnp.logical_not(is_source))
        def _():
            line(i, cols, 1).wait_recv()
            hand_out(i, cols)
            columns_out(i).start()

    n_first = (n_y - 1) * PIECES

    def first(i, carry):
        step(i)
        d, s = i // PIECES + 1, i % PIECES
        rows_arrival(from_y(d), s).wait_recv()
        pass_on(d, s).start()
        return carry

    def later(i, carry):
        step(i)
        return carry

    lax.fori_loop(0, n_first, first, 0)
    units_to(0, twin).start()
    for d in range(1, n_y):
        units_to(d, other_y(d)).start()

    def finish_rows(i, carry):
        group, s = place(i)
        pl.when(jnp.logical_and((i // PIECES) % 2 == 1,
                                jnp.logical_or(jnp.logical_not(is_source), i >= n - n_turns)))(
            lambda: rows_arrival(group, s).wait_recv())
        return carry

    def turn(b):
        part = pl.ds(pl.multiple_of(b * tile, tile), tile)
        rows_t[part, :] = (rows[:, part].T * factor).astype(rows_t.dtype)

    def last(i, carry):
        step(i)
        turn(i - (n - n_turns))
        return carry

    lax.fori_loop(n_first, n - n_turns, later, 0)
    lax.fori_loop(0, n, finish_rows, 0)
    middle = n - max(1, n_turns // 2)
    lax.fori_loop(n - n_turns, middle, last, 0)
    for d in range(1, n_y):
        units_arrival(from_y(d)).wait_recv()
        units_pass(d).start()
    lax.fori_loop(middle, n, last, 0)
    rows_done.start()

    for k in range(n_y):
        units_arrival(lax.rem(y + k, n_y) * 2 + 1 - core).wait_recv()
    own_units.wait()
    units_done.start()
    own, span = mine_t.shape[0], window_t.shape[0]
    first_column = h * own
    start = jnp.minimum(first_column // 128 * 128, units.shape[1] - span)

    def turn_units(b, carry):
        there = pl.ds(pl.multiple_of(start + b * 128, 128), 128)
        window_t[pl.ds(pl.multiple_of(b * 128, 128), 128), :] = (
            units[:, there].T.astype(jnp.float32) * scale)
        return carry

    lax.fori_loop(0, span // 128, turn_units, 0)
    mine_t[...] = window_t[pl.ds(pl.multiple_of(first_column - start, 8), own), :].astype(
        mine_t.dtype)
    mine_done.start()

    def finish(i, carry):
        for d in range(1, q):
            cross_arrival(i, d).wait_recv()
            cross_out(i, d).start()
        return carry

    def finish_sends(i, carry):
        for d in range(1, q):
            cross(i, cols, d).wait_send()
            cross_out(i, d).wait()
        pl.when(goes_up)(lambda: line(i, cols, 1).wait_send())
        pl.when(goes_down)(lambda: line(i, cols, -1).wait_send())
        columns_out(i).wait()
        return carry

    lax.fori_loop(0, n, finish, 0)
    lax.fori_loop(0, n, finish_sends, 0)
    rows_done.wait()
    mine_done.wait()
    units_done.wait()
    for s in range(PIECES):
        to_twin(s).wait_send()
        for d in range(1, n_y):
            to_peer(d, s).wait_send()
            pass_on(d, s).wait_send()
    units_to(0, twin).wait_send()
    for d in range(1, n_y):
        units_to(d, other_y(d)).wait_send()
        units_pass(d).wait_send()


def gather(normed, hidden, scale):
    n_tp, n_hb = lax.axis_size("tp"), lax.axis_size("hb")
    q, n_y = n_tp // n_hb, n_hb // 2
    tokens, width = normed.shape
    units = hidden.shape[1]
    own = units // n_hb
    total = n_hb * tokens
    n = n_hb * PIECES
    dma = pltpu.SemaphoreType.DMA
    anywhere = pl.BlockSpec(memory_space=pltpu.HBM)
    far = max(1, (n_y - 1) * PIECES)
    crossings = max(1, q - 1) * n
    kind = normed.dtype
    return pl.pallas_call(
        functools.partial(gather_kernel, n_tp, n_hb, scale),
        out_shape=(
            jax.ShapeDtypeStruct((width, total), kind),
            jax.ShapeDtypeStruct((own, total), kind),
            jax.ShapeDtypeStruct((total, units), kind),
            jax.ShapeDtypeStruct((total, q * width), kind),
        ),
        in_specs=[anywhere] * 2,
        out_specs=(anywhere,) * 4,
        scratch_shapes=[
            pltpu.VMEM((total, width), kind),
            pltpu.VMEM((total, units), kind),
            pltpu.VMEM((total, q * width), kind),
            pltpu.VMEM((width, total), kind),
            pltpu.VMEM((window_of(own, units), total), jnp.float32),
            pltpu.VMEM((own, total), kind),
            dma((5,)), dma((PIECES,)), dma((far,)), dma((far,)), dma((n,)),
            dma((2 * n_y,)), dma((n_hb,)), dma((2 * n,)), dma((n,)),
            dma((crossings,)), dma((crossings,)), dma((n,)), dma((crossings,)),
        ],
        compiler_params=pltpu.CompilerParams(
            collective_id=0, has_side_effects=True, vmem_limit_bytes=60 * 2**20),
    )(normed, hidden)


def part_of(size, unit, most):
    sizes = [p for p in range(unit, most + 1, unit) if size % p == 0]
    return sizes[-1] if sizes else size


def product_kernel(slots, mine_t, units, rows_t, cols, down, h_in,
                   mine_v, units_v, rows_v, cols_v, down_v, h_in_v,
                   left_sem, units_sem, cols_sem, down_sem, h_in_sem):
    get_mine = pltpu.make_async_copy(mine_t, mine_v, left_sem.at[0])
    get_rows = pltpu.make_async_copy(rows_t, rows_v, left_sem.at[1])

    def get(src, dst, sems, j, wide):
        there = pl.ds(pl.multiple_of(j * wide, 128), wide)
        return pltpu.make_async_copy(src.at[:, there], dst.at[:, there], sems.at[j])

    def product(left, right, right_hbm, right_sems, out, out_v, out_sems):
        high, wide = out_v.shape[1:]
        n_high, n_wide = out.shape[0] // high, out.shape[1] // wide
        n = n_high * n_wide

        def put(i):
            slot = i % slots
            down_by = pl.ds(pl.multiple_of((i % n_high) * high, 8), high)
            along = pl.ds(pl.multiple_of((i // n_high) * wide, 128), wide)
            return pltpu.make_async_copy(out_v.at[slot], out.at[down_by, along], out_sems.at[slot])

        def step(i, carry):
            m, j = i % n_high, i // n_high
            pl.when(m == 0)(lambda: get(right_hbm, right, right_sems, j, wide).wait())
            pl.when(i >= slots)(lambda: put(i - slots).wait())
            rows_here = left[pl.ds(pl.multiple_of(m * high, 8), high), :]
            columns_here = right[:, pl.ds(pl.multiple_of(j * wide, 128), wide)]
            out_v[i % slots] = jnp.dot(
                rows_here, columns_here, preferred_element_type=jnp.float32)
            put(i).start()
            return carry

        lax.fori_loop(0, n, step, 0)
        return [put(i) for i in range(max(0, n - slots), n)]

    units_wide, cols_wide = down_v.shape[2], h_in_v.shape[2]
    get_mine.start()
    for j in range(units.shape[1] // units_wide):
        get(units, units_v, units_sem, j, units_wide).start()
    get_rows.start()
    for j in range(cols.shape[1] // cols_wide):
        get(cols, cols_v, cols_sem, j, cols_wide).start()
    get_mine.wait()
    puts = product(mine_v, units_v, units, units_sem, down, down_v, down_sem)
    get_rows.wait()
    puts += product(rows_v, cols_v, cols, cols_sem, h_in, h_in_v, h_in_sem)
    for put in puts:
        put.wait()


def products(rows_t, mine_t, units, cols):
    own, tokens = mine_t.shape
    high = rows_t.shape[0]
    slots = 4
    down_tile = part_of(own, 16, 512), part_of(units.shape[1], 128, 1664)
    in_tile = part_of(high, 16, 512), part_of(cols.shape[1], 128, 1024)
    in_hbm = pl.BlockSpec(memory_space=pltpu.HBM)
    dma = pltpu.SemaphoreType.DMA
    return pl.pallas_call(
        functools.partial(product_kernel, slots),
        out_shape=(
            jax.ShapeDtypeStruct((own, units.shape[1]), jnp.float32),
            jax.ShapeDtypeStruct((high, cols.shape[1]), jnp.float32),
        ),
        in_specs=[in_hbm] * 4,
        out_specs=(in_hbm,) * 2,
        scratch_shapes=[
            pltpu.VMEM(mine_t.shape, mine_t.dtype),
            pltpu.VMEM(units.shape, units.dtype),
            pltpu.VMEM(rows_t.shape, rows_t.dtype),
            pltpu.VMEM(cols.shape, cols.dtype),
            pltpu.VMEM((slots, *down_tile), jnp.float32),
            pltpu.VMEM((slots, *in_tile), jnp.float32),
            dma((2,)), dma((units.shape[1] // down_tile[1],)),
            dma((cols.shape[1] // in_tile[1],)), dma((slots,)), dma((slots,)),
        ],
        compiler_params=pltpu.CompilerParams(vmem_limit_bytes=60 * 2**20),
    )(mine_t, units, rows_t, cols)


def per_device(normed, hidden):
    total = normed.shape[0] * lax.axis_size("hb")
    assert total & (total - 1) == 0
    rows_t, mine_t, units, cols = gather(normed, hidden, 2.0 / total)
    h_down, h_in = products(rows_t, mine_t, units, cols)
    return (h_in, h_down)


def solution(mesh):
    return jax.shard_map(
        per_device,
        mesh=mesh,
        in_specs=(P("hb", "tp"), P("hb", "tp")),
        out_specs=(P("tp", "hb"), P(("tp", "hb"), None)),
        check_vma=False,
    )
```

```python
import functools

import jax
import jax.numpy as jnp
from jax import lax
from jax.experimental import pallas as pl
from jax.experimental.pallas import tpu as pltpu
from jax.sharding import PartitionSpec as P

MESH = pl.DeviceIdType.MESH
PIECES = 4


def tile_of(width):
    return 256 if width % 256 == 0 else 128


def window_of(own, width):
    return min(width, -(-(own + 120) // 128) * 128)


def gather_kernel(n_tp, n_hb, scale, normed, hidden, rows_out, mine_out, units_out, cols_out,
                  rows, units, cols, rows_t, window_t, mine_t, relayed,
                  local_sem, twin_send, peer_send, pass_send, rows_recv,
                  unit_send, unit_recv, line_send, line_recv, cross_send, cross_recv,
                  out_sem, cross_out_sem, relay_send, relay_recv, over_send):
    q = n_tp // n_hb
    n_y = n_hb // 2
    t, h = lax.axis_index("tp"), lax.axis_index("hb")
    z, x = t // q, t % q
    y, core = h // 2, h % 2
    twin = y * 2 + 1 - core
    tokens, width = normed.shape
    piece = tokens // PIECES
    n = n_hb * PIECES
    is_source = z == h
    goes_up = jnp.logical_and(z >= h, z < n_hb - 1)
    goes_down = jnp.logical_and(z <= h, z > 0)

    half = n // 2
    relief = n_hb == 4
    is_up, is_down = h == 3, h == 0
    relay_source = jnp.logical_or(jnp.logical_and(is_up, z == 1), jnp.logical_and(is_down, z == 2))
    relay_middle = jnp.logical_or(jnp.logical_and(is_up, z == 2), jnp.logical_and(is_down, z == 1))
    relay_end = jnp.logical_or(jnp.logical_and(is_up, z == 3), jnp.logical_and(is_down, z == 0))
    relay_sends = jnp.logical_or(relay_source, relay_middle)
    relay_receives = jnp.logical_or(relay_middle, relay_end)

    def sends_up(i):
        if not relief:
            return goes_up
        return jnp.logical_and(goes_up, jnp.logical_or(h != 1, i < half))

    def sends_down(i):
        if not relief:
            return goes_down
        return jnp.logical_and(goes_down, jnp.logical_or(h != 2, i < half))

    def other_y(d):
        return lax.rem(y + d, n_y) * 2 + core

    def from_y(d):
        return other_y(d)

    def at(group, s):
        return pl.ds(pl.multiple_of(group * tokens + s * piece, piece), piece)

    def block(ref, group):
        return ref.at[pl.ds(pl.multiple_of(group * tokens, tokens), tokens), :]

    def columns(position):
        return pl.ds(pl.multiple_of(position * width, width), width)

    def remote(src, dst, send, recv, where):
        return pltpu.make_async_remote_copy(
            src_ref=src, dst_ref=dst, send_sem=send, recv_sem=recv,
            device_id=where, device_id_type=MESH)

    barrier = pltpu.get_barrier_semaphore()

    def greet(where):
        pl.semaphore_signal(barrier, inc=1, device_id=where, device_id_type=MESH)

    greet({"hb": twin})
    for d in range(1, n_y):
        greet({"hb": other_y(d)})
    for d in range(1, q):
        greet({"tp": z * q + lax.rem(x + d, q)})
    pl.when(z > 0)(lambda: greet({"tp": t - q}))
    pl.when(z < n_hb - 1)(lambda: greet({"tp": t + q}))
    ends = jnp.where(z > 0, 1, 0) + jnp.where(z < n_hb - 1, 1, 0)
    pl.semaphore_wait(barrier, 1 + (n_y - 1) + (q - 1) + ends)

    own_rows = pltpu.make_async_copy(normed, block(rows, h), local_sem.at[0])
    own_units = pltpu.make_async_copy(hidden, block(units, h), local_sem.at[1])

    def own_piece(s):
        return normed.at[pl.ds(pl.multiple_of(s * piece, piece), piece), :]

    def to_twin(s):
        return remote(own_piece(s), rows.at[at(h, s), :], twin_send.at[s],
                      rows_recv.at[h * PIECES + s], {"hb": twin})

    def to_peer(d, s):
        return remote(own_piece(s), rows.at[at(h, s), :], peer_send.at[(d - 1) * PIECES + s],
                      rows_recv.at[h * PIECES + s], {"hb": other_y(d)})

    def pass_on(d, s):
        group = from_y(d)
        return remote(rows.at[at(group, s), :], rows.at[at(group, s), :],
                      pass_send.at[(d - 1) * PIECES + s],
                      rows_recv.at[group * PIECES + s], {"hb": twin})

    def rows_arrival(group, s):
        return remote(own_piece(s), rows.at[at(group, s), :], twin_send.at[s],
                      rows_recv.at[group * PIECES + s], {"hb": twin})

    def units_to(i, where):
        return remote(hidden, block(units, h), unit_send.at[i], unit_recv.at[h], {"hb": where})

    def units_pass(d):
        group = from_y(d)
        return remote(block(units, group), block(units, group), unit_send.at[n_y - 1 + d],
                      unit_recv.at[group], {"hb": twin})

    def units_arrival(group):
        return remote(hidden, block(units, group), unit_send.at[0], unit_recv.at[group],
                      {"hb": twin})

    def place(i):
        k, s = i // PIECES, i % PIECES
        hy, hc = k // 2, k % 2
        group = lax.rem(y + hy, n_y) * 2 + lax.rem(core + hc, 2)
        return group, s

    def line(i, src, step):
        group, s = place(i)
        return remote(src.at[at(group, s), columns(x) if src is cols else slice(None)],
                      cols.at[at(group, s), columns(x)],
                      line_send.at[(0 if step < 0 else n) + i], line_recv.at[i],
                      {"tp": t + step * q})

    def cross(i, src, d):
        group, s = place(i)
        return remote(src.at[at(group, s), columns(x) if src is cols else slice(None)],
                      cols.at[at(group, s), columns(x)],
                      cross_send.at[(d - 1) * n + i], cross_recv.at[(d - 1) * n + i],
                      {"tp": z * q + lax.rem(x + d, q)})

    def cross_arrival(i, d):
        group, s = place(i)
        there = cols.at[at(group, s), columns(lax.rem(x - d + q, q))]
        return remote(there, there, cross_send.at[(d - 1) * n + i],
                      cross_recv.at[(d - 1) * n + i], {"tp": z * q + lax.rem(x + d, q)})

    def columns_out(i):
        group, s = place(i)
        there = at(group, s), columns(x)
        return pltpu.make_async_copy(cols.at[there], cols_out.at[there], out_sem.at[i])

    def own_columns_out(i):
        group, s = place(i)
        return pltpu.make_async_copy(rows.at[at(group, s), :],
                                     cols_out.at[at(group, s), columns(x)], out_sem.at[i])

    def cross_out(i, d):
        group, s = place(i)
        there = at(group, s), columns(lax.rem(x - d + q, q))
        return pltpu.make_async_copy(cols.at[there], cols_out.at[there],
                                     cross_out_sem.at[(d - 1) * n + i])

    rows_done = pltpu.make_async_copy(rows_t, rows_out, local_sem.at[2])
    mine_done = pltpu.make_async_copy(mine_t, mine_out, local_sem.at[3])
    units_done = pltpu.make_async_copy(units, units_out, local_sem.at[4])

    own_rows.start()
    for d in range(1, n_y):
        for s in range(PIECES):
            to_peer(d, s).start()
    for s in range(PIECES):
        to_twin(s).start()
    own_units.start()
    own_rows.wait()

    tile = tile_of(width)
    n_turns = width // tile
    factor = jnp.asarray(scale, rows_t.dtype)

    def hand_out(i, src):
        pl.when(sends_up(i))(lambda: line(i, src, 1).start())
        pl.when(sends_down(i))(lambda: line(i, src, -1).start())
        for d in range(1, q):
            cross(i, src, d).start()

    def relay_piece(r):
        return relayed.at[pl.ds(pl.multiple_of(r * piece, piece), piece), :]

    def relay(r, src):
        return remote(src, relay_piece(r), relay_send.at[r], relay_recv.at[r],
                      {"tp": t + jnp.where(is_up, q, -q)})

    def over(r):
        group = y * 2 + lax.rem(core + r // PIECES, 2)
        return remote(relay_piece(r), cols.at[at(group, r % PIECES), columns(x)],
                      over_send.at[r], line_recv.at[half + r], {"hb": other_y(1)})

    def relay_step(r):
        @pl.when(relay_receives)
        def _():
            relay(r, relay_piece(r)).wait_recv()
            pl.when(relay_middle)(lambda: relay(r, relay_piece(r)).start())
            over(r).start()

    if relief:
        @pl.when(relay_source)
        def _():
            for s in range(PIECES):
                relay(s, own_piece(s)).start()
            for s in range(PIECES):
                rows_arrival(twin, s).wait_recv()
                relay(PIECES + s, rows.at[at(twin, s), :]).start()

    def step(i):
        group, s = place(i)

        @pl.when(is_source)
        def _():
            awaited = jnp.logical_and(i < n - n_turns, (i // PIECES) % 2 == 1)
            pl.when(awaited)(lambda: rows_arrival(group, s).wait_recv())
            hand_out(i, rows)
            own_columns_out(i).start()

        @pl.when(jnp.logical_not(is_source))
        def _():
            line(i, cols, 1).wait_recv()
            hand_out(i, cols)
            columns_out(i).start()

    n_first = (n_y - 1) * PIECES

    def first(i, carry):
        step(i)
        d, s = i // PIECES, i % PIECES
        rows_arrival(from_y(d), s).wait_recv()
        pass_on(d, s).start()
        if relief:
            relay_step(i - PIECES)
        return carry

    def later(i, carry):
        step(i)
        if relief:
            pl.when(jnp.logical_and(i >= PIECES, i < PIECES + half))(
                lambda: relay_step(i - PIECES))
        return carry

    lax.fori_loop(0, PIECES, later, 0)
    lax.fori_loop(PIECES, PIECES + n_first, first, 0)
    units_to(0, twin).start()
    for d in range(1, n_y):
        units_to(d, other_y(d)).start()

    def finish_rows(i, carry):
        group, s = place(i)
        awaited = jnp.logical_and((i // PIECES) % 2 == 1,
                                  jnp.logical_or(jnp.logical_not(is_source), i >= n - n_turns))
        if relief:
            awaited = jnp.logical_and(awaited, jnp.logical_or(jnp.logical_not(relay_source),
                                                              i >= half))
        pl.when(awaited)(lambda: rows_arrival(group, s).wait_recv())
        return carry

    def turn(b):
        part = pl.ds(pl.multiple_of(b * tile, tile), tile)
        rows_t[part, :] = (rows[:, part].T * factor).astype(rows_t.dtype)

    def last(i, carry):
        step(i)
        if relief:
            pl.when(i < PIECES + half)(lambda: relay_step(i - PIECES))
        turn(i - (n - n_turns))
        return carry

    lax.fori_loop(PIECES + n_first, n - n_turns, later, 0)
    lax.fori_loop(0, n, finish_rows, 0)
    middle = n - max(1, n_turns // 2)
    lax.fori_loop(n - n_turns, middle, last, 0)
    for d in range(1, n_y):
        units_arrival(from_y(d)).wait_recv()
        units_pass(d).start()
    lax.fori_loop(middle, n, last, 0)
    rows_done.start()

    for k in range(n_y):
        units_arrival(lax.rem(y + k, n_y) * 2 + 1 - core).wait_recv()
    own_units.wait()
    units_done.start()
    own, span = mine_t.shape[0], window_t.shape[0]
    first_column = h * own
    start = jnp.minimum(first_column // 128 * 128, units.shape[1] - span)

    def turn_units(b, carry):
        there = pl.ds(pl.multiple_of(start + b * 128, 128), 128)
        window_t[pl.ds(pl.multiple_of(b * 128, 128), 128), :] = (
            units[:, there].T.astype(jnp.float32) * scale)
        return carry

    lax.fori_loop(0, span // 128, turn_units, 0)
    mine_t[...] = window_t[pl.ds(pl.multiple_of(first_column - start, 8), own), :].astype(
        mine_t.dtype)
    mine_done.start()

    def finish(i, carry):
        for d in range(1, q):
            cross_arrival(i, d).wait_recv()
            cross_out(i, d).start()
        return carry

    def finish_sends(i, carry):
        for d in range(1, q):
            cross(i, cols, d).wait_send()
            cross_out(i, d).wait()
        pl.when(sends_up(i))(lambda: line(i, cols, 1).wait_send())
        pl.when(sends_down(i))(lambda: line(i, cols, -1).wait_send())
        columns_out(i).wait()
        return carry

    lax.fori_loop(0, n, finish, 0)
    lax.fori_loop(0, n, finish_sends, 0)

    def finish_relay(r, carry):
        pl.when(relay_sends)(lambda: relay(r, relay_piece(r)).wait_send())
        pl.when(relay_receives)(lambda: over(r).wait_send())
        return carry

    if relief:
        lax.fori_loop(0, half, finish_relay, 0)
    rows_done.wait()
    mine_done.wait()
    units_done.wait()
    for s in range(PIECES):
        to_twin(s).wait_send()
        for d in range(1, n_y):
            to_peer(d, s).wait_send()
            pass_on(d, s).wait_send()
    units_to(0, twin).wait_send()
    for d in range(1, n_y):
        units_to(d, other_y(d)).wait_send()
        units_pass(d).wait_send()


def gather(normed, hidden, scale):
    n_tp, n_hb = lax.axis_size("tp"), lax.axis_size("hb")
    q, n_y = n_tp // n_hb, n_hb // 2
    tokens, width = normed.shape
    units = hidden.shape[1]
    own = units // n_hb
    total = n_hb * tokens
    n = n_hb * PIECES
    dma = pltpu.SemaphoreType.DMA
    anywhere = pl.BlockSpec(memory_space=pltpu.HBM)
    far = max(1, (n_y - 1) * PIECES)
    crossings = max(1, q - 1) * n
    kind = normed.dtype
    return pl.pallas_call(
        functools.partial(gather_kernel, n_tp, n_hb, scale),
        out_shape=(
            jax.ShapeDtypeStruct((width, total), kind),
            jax.ShapeDtypeStruct((own, total), kind),
            jax.ShapeDtypeStruct((total, units), kind),
            jax.ShapeDtypeStruct((total, q * width), kind),
        ),
        in_specs=[anywhere] * 2,
        out_specs=(anywhere,) * 4,
        scratch_shapes=[
            pltpu.VMEM((total, width), kind),
            pltpu.VMEM((total, units), kind),
            pltpu.VMEM((total, q * width), kind),
            pltpu.VMEM((width, total), kind),
            pltpu.VMEM((window_of(own, units), total), jnp.float32),
            pltpu.VMEM((own, total), kind),
            pltpu.VMEM((total // 2, width), kind),
            dma((5,)), dma((PIECES,)), dma((far,)), dma((far,)), dma((n,)),
            dma((2 * n_y,)), dma((n_hb,)), dma((2 * n,)), dma((n,)),
            dma((crossings,)), dma((crossings,)), dma((n,)), dma((crossings,)),
            dma((n // 2,)), dma((n // 2,)), dma((n // 2,)),
        ],
        compiler_params=pltpu.CompilerParams(
            collective_id=0, has_side_effects=True, vmem_limit_bytes=60 * 2**20),
    )(normed, hidden)


def part_of(size, unit, most):
    sizes = [p for p in range(unit, most + 1, unit) if size % p == 0]
    return sizes[-1] if sizes else size


def product_kernel(slots, mine_t, units, rows_t, cols, down, h_in,
                   mine_v, units_v, rows_v, cols_v, down_v, h_in_v,
                   left_sem, units_sem, cols_sem, down_sem, h_in_sem):
    get_mine = pltpu.make_async_copy(mine_t, mine_v, left_sem.at[0])
    get_rows = pltpu.make_async_copy(rows_t, rows_v, left_sem.at[1])

    def get(src, dst, sems, j, wide):
        there = pl.ds(pl.multiple_of(j * wide, 128), wide)
        return pltpu.make_async_copy(src.at[:, there], dst.at[:, there], sems.at[j])

    def product(left, right, right_hbm, right_sems, out, out_v, out_sems):
        high, wide = out_v.shape[1:]
        n_high, n_wide = out.shape[0] // high, out.shape[1] // wide
        n = n_high * n_wide

        def put(i):
            slot = i % slots
            down_by = pl.ds(pl.multiple_of((i % n_high) * high, 8), high)
            along = pl.ds(pl.multiple_of((i // n_high) * wide, 128), wide)
            return pltpu.make_async_copy(out_v.at[slot], out.at[down_by, along], out_sems.at[slot])

        def step(i, carry):
            m, j = i % n_high, i // n_high
            pl.when(m == 0)(lambda: get(right_hbm, right, right_sems, j, wide).wait())
            pl.when(i >= slots)(lambda: put(i - slots).wait())
            rows_here = left[pl.ds(pl.multiple_of(m * high, 8), high), :]
            columns_here = right[:, pl.ds(pl.multiple_of(j * wide, 128), wide)]
            out_v[i % slots] = jnp.dot(
                rows_here, columns_here, preferred_element_type=jnp.float32)
            put(i).start()
            return carry

        lax.fori_loop(0, n, step, 0)
        return [put(i) for i in range(max(0, n - slots), n)]

    units_wide, cols_wide = down_v.shape[2], h_in_v.shape[2]
    get_mine.start()
    for j in range(units.shape[1] // units_wide):
        get(units, units_v, units_sem, j, units_wide).start()
    get_rows.start()
    for j in range(cols.shape[1] // cols_wide):
        get(cols, cols_v, cols_sem, j, cols_wide).start()
    get_mine.wait()
    puts = product(mine_v, units_v, units, units_sem, down, down_v, down_sem)
    get_rows.wait()
    puts += product(rows_v, cols_v, cols, cols_sem, h_in, h_in_v, h_in_sem)
    for put in puts:
        put.wait()


def products(rows_t, mine_t, units, cols):
    own, tokens = mine_t.shape
    high = rows_t.shape[0]
    slots = 4
    down_tile = part_of(own, 16, 512), part_of(units.shape[1], 128, 1664)
    in_tile = part_of(high, 16, 512), part_of(cols.shape[1], 128, 1024)
    in_hbm = pl.BlockSpec(memory_space=pltpu.HBM)
    dma = pltpu.SemaphoreType.DMA
    return pl.pallas_call(
        functools.partial(product_kernel, slots),
        out_shape=(
            jax.ShapeDtypeStruct((own, units.shape[1]), jnp.float32),
            jax.ShapeDtypeStruct((high, cols.shape[1]), jnp.float32),
        ),
        in_specs=[in_hbm] * 4,
        out_specs=(in_hbm,) * 2,
        scratch_shapes=[
            pltpu.VMEM(mine_t.shape, mine_t.dtype),
            pltpu.VMEM(units.shape, units.dtype),
            pltpu.VMEM(rows_t.shape, rows_t.dtype),
            pltpu.VMEM(cols.shape, cols.dtype),
            pltpu.VMEM((slots, *down_tile), jnp.float32),
            pltpu.VMEM((slots, *in_tile), jnp.float32),
            dma((2,)), dma((units.shape[1] // down_tile[1],)),
            dma((cols.shape[1] // in_tile[1],)), dma((slots,)), dma((slots,)),
        ],
        compiler_params=pltpu.CompilerParams(vmem_limit_bytes=60 * 2**20),
    )(mine_t, units, rows_t, cols)


def per_device(normed, hidden):
    total = normed.shape[0] * lax.axis_size("hb")
    assert total & (total - 1) == 0
    rows_t, mine_t, units, cols = gather(normed, hidden, 2.0 / total)
    h_down, h_in = products(rows_t, mine_t, units, cols)
    return (h_in, h_down)


def solution(mesh):
    return jax.shard_map(
        per_device,
        mesh=mesh,
        in_specs=(P("hb", "tp"), P("hb", "tp")),
        out_specs=(P("tp", "hb"), P(("tp", "hb"), None)),
        check_vma=False,
    )
```

```python
import functools

import jax
import jax.numpy as jnp
from jax import lax
from jax.experimental import pallas as pl
from jax.experimental.pallas import tpu as pltpu
from jax.sharding import PartitionSpec as P

MESH = pl.DeviceIdType.MESH
PIECES = 4


def tile_of(width):
    return 256 if width % 256 == 0 else 128


def window_of(own, width):
    return min(width, -(-(own + 120) // 128) * 128)


def gather_kernel(n_tp, n_hb, scale, normed, hidden, rows_out, mine_out, units_out, cols_out,
                  rows, units, cols, rows_t, window_t, mine_t, relayed,
                  local_sem, twin_send, peer_send, pass_send, rows_recv,
                  unit_send, unit_recv, line_send, line_recv, cross_send, cross_recv,
                  out_sem, cross_out_sem, relay_send, relay_recv, over_send):
    q = n_tp // n_hb
    n_y = n_hb // 2
    t, h = lax.axis_index("tp"), lax.axis_index("hb")
    z, x = t // q, t % q
    y, core = h // 2, h % 2
    twin = y * 2 + 1 - core
    tokens, width = normed.shape
    piece = tokens // PIECES
    n = n_hb * PIECES
    is_source = z == h
    goes_up = jnp.logical_and(z >= h, z < n_hb - 1)
    goes_down = jnp.logical_and(z <= h, z > 0)

    half = n // 2
    relief = n_hb == 4
    is_up, is_down = h == 3, h == 0
    relay_source = jnp.logical_or(jnp.logical_and(is_up, z == 1), jnp.logical_and(is_down, z == 2))
    relay_middle = jnp.logical_or(jnp.logical_and(is_up, z == 2), jnp.logical_and(is_down, z == 1))
    relay_end = jnp.logical_or(jnp.logical_and(is_up, z == 3), jnp.logical_and(is_down, z == 0))
    relay_sends = jnp.logical_or(relay_source, relay_middle)
    relay_receives = jnp.logical_or(relay_middle, relay_end)

    def sends_up(i):
        if not relief:
            return goes_up
        return jnp.logical_and(goes_up, jnp.logical_or(h != 1, i // PIECES != 2))

    def sends_down(i):
        if not relief:
            return goes_down
        return jnp.logical_and(goes_down, jnp.logical_or(h != 2, i // PIECES != 2))

    def other_y(d):
        return lax.rem(y + d, n_y) * 2 + core

    def from_y(d):
        return other_y(d)

    def at(group, s):
        return pl.ds(pl.multiple_of(group * tokens + s * piece, piece), piece)

    def block(ref, group):
        return ref.at[pl.ds(pl.multiple_of(group * tokens, tokens), tokens), :]

    def columns(position):
        return pl.ds(pl.multiple_of(position * width, width), width)

    def remote(src, dst, send, recv, where):
        return pltpu.make_async_remote_copy(
            src_ref=src, dst_ref=dst, send_sem=send, recv_sem=recv,
            device_id=where, device_id_type=MESH)

    barrier = pltpu.get_barrier_semaphore()

    def greet(where):
        pl.semaphore_signal(barrier, inc=1, device_id=where, device_id_type=MESH)

    greet({"hb": twin})
    for d in range(1, n_y):
        greet({"hb": other_y(d)})
    for d in range(1, q):
        greet({"tp": z * q + lax.rem(x + d, q)})
    pl.when(z > 0)(lambda: greet({"tp": t - q}))
    pl.when(z < n_hb - 1)(lambda: greet({"tp": t + q}))
    ends = jnp.where(z > 0, 1, 0) + jnp.where(z < n_hb - 1, 1, 0)
    pl.semaphore_wait(barrier, 1 + (n_y - 1) + (q - 1) + ends)

    own_rows = pltpu.make_async_copy(normed, block(rows, h), local_sem.at[0])
    own_units = pltpu.make_async_copy(hidden, block(units, h), local_sem.at[1])

    def own_piece(s):
        return normed.at[pl.ds(pl.multiple_of(s * piece, piece), piece), :]

    def to_twin(s):
        return remote(own_piece(s), rows.at[at(h, s), :], twin_send.at[s],
                      rows_recv.at[h * PIECES + s], {"hb": twin})

    def to_peer(d, s):
        return remote(own_piece(s), rows.at[at(h, s), :], peer_send.at[(d - 1) * PIECES + s],
                      rows_recv.at[h * PIECES + s], {"hb": other_y(d)})

    def pass_on(d, s):
        group = from_y(d)
        return remote(rows.at[at(group, s), :], rows.at[at(group, s), :],
                      pass_send.at[(d - 1) * PIECES + s],
                      rows_recv.at[group * PIECES + s], {"hb": twin})

    def rows_arrival(group, s):
        return remote(own_piece(s), rows.at[at(group, s), :], twin_send.at[s],
                      rows_recv.at[group * PIECES + s], {"hb": twin})

    def units_to(i, where):
        return remote(hidden, block(units, h), unit_send.at[i], unit_recv.at[h], {"hb": where})

    def units_pass(d):
        group = from_y(d)
        return remote(block(units, group), block(units, group), unit_send.at[n_y - 1 + d],
                      unit_recv.at[group], {"hb": twin})

    def units_arrival(group):
        return remote(hidden, block(units, group), unit_send.at[0], unit_recv.at[group],
                      {"hb": twin})

    def place(i):
        k, s = i // PIECES, i % PIECES
        hy, hc = k // 2, k % 2
        group = lax.rem(y + hy, n_y) * 2 + lax.rem(core + hc, 2)
        return group, s

    def line(i, src, step):
        group, s = place(i)
        return remote(src.at[at(group, s), columns(x) if src is cols else slice(None)],
                      cols.at[at(group, s), columns(x)],
                      line_send.at[(0 if step < 0 else n) + i], line_recv.at[i],
                      {"tp": t + step * q})

    def cross(i, src, d):
        group, s = place(i)
        return remote(src.at[at(group, s), columns(x) if src is cols else slice(None)],
                      cols.at[at(group, s), columns(x)],
                      cross_send.at[(d - 1) * n + i], cross_recv.at[(d - 1) * n + i],
                      {"tp": z * q + lax.rem(x + d, q)})

    def cross_arrival(i, d):
        group, s = place(i)
        there = cols.at[at(group, s), columns(lax.rem(x - d + q, q))]
        return remote(there, there, cross_send.at[(d - 1) * n + i],
                      cross_recv.at[(d - 1) * n + i], {"tp": z * q + lax.rem(x + d, q)})

    def columns_out(i):
        group, s = place(i)
        there = at(group, s), columns(x)
        return pltpu.make_async_copy(cols.at[there], cols_out.at[there], out_sem.at[i])

    def own_columns_out(i):
        group, s = place(i)
        return pltpu.make_async_copy(rows.at[at(group, s), :],
                                     cols_out.at[at(group, s), columns(x)], out_sem.at[i])

    def cross_out(i, d):
        group, s = place(i)
        there = at(group, s), columns(lax.rem(x - d + q, q))
        return pltpu.make_async_copy(cols.at[there], cols_out.at[there],
                                     cross_out_sem.at[(d - 1) * n + i])

    rows_done = pltpu.make_async_copy(rows_t, rows_out, local_sem.at[2])
    mine_done = pltpu.make_async_copy(mine_t, mine_out, local_sem.at[3])
    units_done = pltpu.make_async_copy(units, units_out, local_sem.at[4])

    own_rows.start()
    for d in range(1, n_y):
        for s in range(PIECES):
            to_peer(d, s).start()
    for s in range(PIECES):
        to_twin(s).start()
    own_units.start()
    own_rows.wait()

    tile = tile_of(width)
    n_turns = width // tile
    factor = jnp.asarray(scale, rows_t.dtype)

    def hand_out(i, src):
        pl.when(sends_up(i))(lambda: line(i, src, 1).start())
        pl.when(sends_down(i))(lambda: line(i, src, -1).start())
        for d in range(1, q):
            cross(i, src, d).start()

    def relay_piece(r):
        return relayed.at[pl.ds(pl.multiple_of(r * piece, piece), piece), :]

    def relay(r, src):
        return remote(src, relay_piece(r), relay_send.at[r], relay_recv.at[r],
                      {"tp": t + jnp.where(is_up, q, -q)})

    def over(r):
        return remote(relay_piece(r), cols.at[at(h, r), columns(x)],
                      over_send.at[r], line_recv.at[half + r], {"hb": other_y(1)})

    def relay_step(r):
        @pl.when(relay_receives)
        def _():
            relay(r, relay_piece(r)).wait_recv()
            pl.when(relay_middle)(lambda: relay(r, relay_piece(r)).start())
            over(r).start()

    if relief:
        @pl.when(relay_source)
        def _():
            for s in range(PIECES):
                relay(s, own_piece(s)).start()

    def step(i):
        group, s = place(i)

        @pl.when(is_source)
        def _():
            awaited = jnp.logical_and(i < n - n_turns, (i // PIECES) % 2 == 1)
            pl.when(awaited)(lambda: rows_arrival(group, s).wait_recv())
            hand_out(i, rows)
            own_columns_out(i).start()

        @pl.when(jnp.logical_not(is_source))
        def _():
            line(i, cols, 1).wait_recv()
            hand_out(i, cols)
            columns_out(i).start()

    n_first = (n_y - 1) * PIECES

    def first(i, carry):
        step(i)
        d, s = i // PIECES, i % PIECES
        rows_arrival(from_y(d), s).wait_recv()
        pass_on(d, s).start()
        if relief:
            relay_step(i - PIECES)
        return carry

    def later(i, carry):
        step(i)
        return carry

    lax.fori_loop(0, PIECES, later, 0)
    for d in range(1, n_y):
        units_to(d, other_y(d)).start()
    units_to(0, twin).start()
    lax.fori_loop(PIECES, PIECES + n_first, first, 0)

    def finish_rows(i, carry):
        group, s = place(i)
        awaited = jnp.logical_and((i // PIECES) % 2 == 1,
                                  jnp.logical_or(jnp.logical_not(is_source), i >= n - n_turns))
        pl.when(awaited)(lambda: rows_arrival(group, s).wait_recv())
        return carry

    def turn(b):
        part = pl.ds(pl.multiple_of(b * tile, tile), tile)
        rows_t[part, :] = (rows[:, part].T * factor).astype(rows_t.dtype)

    def last(i, carry):
        step(i)
        turn(i - (n - n_turns))
        return carry

    lax.fori_loop(PIECES + n_first, n - n_turns, later, 0)
    lax.fori_loop(0, n, finish_rows, 0)
    lax.fori_loop(n - n_turns, n, last, 0)
    for d in range(1, n_y):
        units_arrival(from_y(d)).wait_recv()
        units_pass(d).start()
    rows_done.start()

    for k in range(n_y):
        units_arrival(lax.rem(y + k, n_y) * 2 + 1 - core).wait_recv()
    own_units.wait()
    units_done.start()
    own, span = mine_t.shape[0], window_t.shape[0]
    first_column = h * own
    start = jnp.minimum(first_column // 128 * 128, units.shape[1] - span)

    def turn_units(b, carry):
        there = pl.ds(pl.multiple_of(start + b * 128, 128), 128)
        window_t[pl.ds(pl.multiple_of(b * 128, 128), 128), :] = (
            units[:, there].T.astype(jnp.float32) * scale)
        return carry

    lax.fori_loop(0, span // 128, turn_units, 0)
    mine_t[...] = window_t[pl.ds(pl.multiple_of(first_column - start, 8), own), :].astype(
        mine_t.dtype)
    mine_done.start()

    def finish(i, carry):
        for d in range(1, q):
            cross_arrival(i, d).wait_recv()
            cross_out(i, d).start()
        return carry

    def finish_sends(i, carry):
        for d in range(1, q):
            cross(i, cols, d).wait_send()
            cross_out(i, d).wait()
        pl.when(sends_up(i))(lambda: line(i, cols, 1).wait_send())
        pl.when(sends_down(i))(lambda: line(i, cols, -1).wait_send())
        columns_out(i).wait()
        return carry

    lax.fori_loop(0, n, finish, 0)
    lax.fori_loop(0, n, finish_sends, 0)

    def finish_relay(r, carry):
        pl.when(relay_sends)(lambda: relay(r, relay_piece(r)).wait_send())
        pl.when(relay_receives)(lambda: over(r).wait_send())
        return carry

    if relief:
        lax.fori_loop(0, PIECES, finish_relay, 0)
    rows_done.wait()
    mine_done.wait()
    units_done.wait()
    for s in range(PIECES):
        to_twin(s).wait_send()
        for d in range(1, n_y):
            to_peer(d, s).wait_send()
            pass_on(d, s).wait_send()
    units_to(0, twin).wait_send()
    for d in range(1, n_y):
        units_to(d, other_y(d)).wait_send()
        units_pass(d).wait_send()


def gather(normed, hidden, scale):
    n_tp, n_hb = lax.axis_size("tp"), lax.axis_size("hb")
    q, n_y = n_tp // n_hb, n_hb // 2
    tokens, width = normed.shape
    units = hidden.shape[1]
    own = units // n_hb
    total = n_hb * tokens
    n = n_hb * PIECES
    dma = pltpu.SemaphoreType.DMA
    anywhere = pl.BlockSpec(memory_space=pltpu.HBM)
    far = max(1, (n_y - 1) * PIECES)
    crossings = max(1, q - 1) * n
    kind = normed.dtype
    return pl.pallas_call(
        functools.partial(gather_kernel, n_tp, n_hb, scale),
        out_shape=(
            jax.ShapeDtypeStruct((width, total), kind),
            jax.ShapeDtypeStruct((own, total), kind),
            jax.ShapeDtypeStruct((total, units), kind),
            jax.ShapeDtypeStruct((total, q * width), kind),
        ),
        in_specs=[anywhere] * 2,
        out_specs=(anywhere,) * 4,
        scratch_shapes=[
            pltpu.VMEM((total, width), kind),
            pltpu.VMEM((total, units), kind),
            pltpu.VMEM((total, q * width), kind),
            pltpu.VMEM((width, total), kind),
            pltpu.VMEM((window_of(own, units), total), jnp.float32),
            pltpu.VMEM((own, total), kind),
            pltpu.VMEM((tokens, width), kind),
            dma((5,)), dma((PIECES,)), dma((far,)), dma((far,)), dma((n,)),
            dma((2 * n_y,)), dma((n_hb,)), dma((2 * n,)), dma((n,)),
            dma((crossings,)), dma((crossings,)), dma((n,)), dma((crossings,)),
            dma((PIECES,)), dma((PIECES,)), dma((PIECES,)),
        ],
        compiler_params=pltpu.CompilerParams(
            collective_id=0, has_side_effects=True, vmem_limit_bytes=60 * 2**20),
    )(normed, hidden)


def part_of(size, unit, most):
    sizes = [p for p in range(unit, most + 1, unit) if size % p == 0]
    return sizes[-1] if sizes else size


def product_kernel(slots, mine_t, units, rows_t, cols, down, h_in,
                   mine_v, units_v, rows_v, cols_v, down_v, h_in_v,
                   left_sem, units_sem, cols_sem, down_sem, h_in_sem):
    get_mine = pltpu.make_async_copy(mine_t, mine_v, left_sem.at[0])
    get_rows = pltpu.make_async_copy(rows_t, rows_v, left_sem.at[1])

    def get(src, dst, sems, j, wide):
        there = pl.ds(pl.multiple_of(j * wide, 128), wide)
        return pltpu.make_async_copy(src.at[:, there], dst.at[:, there], sems.at[j])

    def product(left, right, right_hbm, right_sems, out, out_v, out_sems):
        high, wide = out_v.shape[1:]
        n_high, n_wide = out.shape[0] // high, out.shape[1] // wide
        n = n_high * n_wide

        def put(i):
            slot = i % slots
            down_by = pl.ds(pl.multiple_of((i % n_high) * high, 8), high)
            along = pl.ds(pl.multiple_of((i // n_high) * wide, 128), wide)
            return pltpu.make_async_copy(out_v.at[slot], out.at[down_by, along], out_sems.at[slot])

        def step(i, carry):
            m, j = i % n_high, i // n_high
            pl.when(m == 0)(lambda: get(right_hbm, right, right_sems, j, wide).wait())
            pl.when(i >= slots)(lambda: put(i - slots).wait())
            rows_here = left[pl.ds(pl.multiple_of(m * high, 8), high), :]
            columns_here = right[:, pl.ds(pl.multiple_of(j * wide, 128), wide)]
            out_v[i % slots] = jnp.dot(
                rows_here, columns_here, preferred_element_type=jnp.float32)
            put(i).start()
            return carry

        lax.fori_loop(0, n, step, 0)
        return [put(i) for i in range(max(0, n - slots), n)]

    units_wide, cols_wide = down_v.shape[2], h_in_v.shape[2]
    get_mine.start()
    for j in range(units.shape[1] // units_wide):
        get(units, units_v, units_sem, j, units_wide).start()
    get_rows.start()
    for j in range(cols.shape[1] // cols_wide):
        get(cols, cols_v, cols_sem, j, cols_wide).start()
    get_mine.wait()
    puts = product(mine_v, units_v, units, units_sem, down, down_v, down_sem)
    get_rows.wait()
    puts += product(rows_v, cols_v, cols, cols_sem, h_in, h_in_v, h_in_sem)
    for put in puts:
        put.wait()


def products(rows_t, mine_t, units, cols):
    own, tokens = mine_t.shape
    high = rows_t.shape[0]
    slots = 4
    down_tile = part_of(own, 16, 512), part_of(units.shape[1], 128, 1664)
    in_tile = part_of(high, 16, 512), part_of(cols.shape[1], 128, 1024)
    in_hbm = pl.BlockSpec(memory_space=pltpu.HBM)
    dma = pltpu.SemaphoreType.DMA
    return pl.pallas_call(
        functools.partial(product_kernel, slots),
        out_shape=(
            jax.ShapeDtypeStruct((own, units.shape[1]), jnp.float32),
            jax.ShapeDtypeStruct((high, cols.shape[1]), jnp.float32),
        ),
        in_specs=[in_hbm] * 4,
        out_specs=(in_hbm,) * 2,
        scratch_shapes=[
            pltpu.VMEM(mine_t.shape, mine_t.dtype),
            pltpu.VMEM(units.shape, units.dtype),
            pltpu.VMEM(rows_t.shape, rows_t.dtype),
            pltpu.VMEM(cols.shape, cols.dtype),
            pltpu.VMEM((slots, *down_tile), jnp.float32),
            pltpu.VMEM((slots, *in_tile), jnp.float32),
            dma((2,)), dma((units.shape[1] // down_tile[1],)),
            dma((cols.shape[1] // in_tile[1],)), dma((slots,)), dma((slots,)),
        ],
        compiler_params=pltpu.CompilerParams(vmem_limit_bytes=60 * 2**20),
    )(mine_t, units, rows_t, cols)


def per_device(normed, hidden):
    total = normed.shape[0] * lax.axis_size("hb")
    assert total & (total - 1) == 0
    rows_t, mine_t, units, cols = gather(normed, hidden, 2.0 / total)
    h_down, h_in = products(rows_t, mine_t, units, cols)
    return (h_in, h_down)


def solution(mesh):
    return jax.shard_map(
        per_device,
        mesh=mesh,
        in_specs=(P("hb", "tp"), P("hb", "tp")),
        out_specs=(P("tp", "hb"), P(("tp", "hb"), None)),
        check_vma=False,
    )
```
